512 devices in a mesh: row: 32 (over x, y), col: 16 (over z, core).
Axes of the slice: x: 4, y: 8, z: 8, core: 2. Of those that a mesh axis runs over, the one named last changes fastest.
Arguments:
- grads_out: bfloat16 [1024, 28672], P('row', 'col'), may hold values from -6 to 6
- acts: bfloat16 [1024, 8192], P('col', 'row'), may hold values from -6 to 6
- query_index: int32 [8], replicated, may hold values from 0 to 1023
- train_index: int32 [384], replicated, may hold values from 0 to 1023
- out_basis: bfloat16 [28672, 28672], P('col', 'row'), may hold values from -0.03125 to 0.03125
- in_basis: bfloat16 [8192, 8192], P('row', 'col'), may hold values from -0.0625 to 0.0625
- eig_products: bfloat16 [28672, 8192], P('row', 'col'), may hold values from 0.5 to 200
Outputs:
- scores: float32 [8, 384], replicated
The draws below stay inside these ranges and needn't reach their ends.
All inputs are finite; a program needn't handle non-finite values.
Results may differ from the reference program's by a relative error of at most 0.0003.
Values may be sent and summed in bfloat16 or wider, within the bound.
A program may use at most 64 MiB of HBM per device.

```python
import math
import jax
import jax.numpy as jnp
from jax import lax

DOUT = 28672
DIN = 8192
QUERIES = 8
TRAIN = 384
POOL = 1024
N_ROW = 32


def draw_indices(key, amount, upper):
    key_values, key_first, key_second = jax.random.split(key, 3)
    drawn = jax.random.randint(key_values, (amount,), 0, upper, dtype=jnp.int32)
    first_spot = jax.random.randint(key_first, (), 0, amount, dtype=jnp.int32)
    second_spot = (first_spot + 1 + jax.random.randint(key_second, (), 0, amount - 1, dtype=jnp.int32)) % amount
    places = jnp.arange(amount, dtype=jnp.int32)
    drawn = jnp.where(places == first_spot, upper - 1, drawn)
    drawn = jnp.where(places == second_spot, 0, drawn)
    return drawn


def draw_query_index(key, part):
    key = jax.random.fold_in(key, 11)
    return draw_indices(key, QUERIES, POOL)


def draw_train_index(key, part):
    key = jax.random.fold_in(key, 12)
    return draw_indices(key, TRAIN, POOL)


def draw_eig_products(key, part):
    key = jax.random.fold_in(key, 21)
    key_entry, key_column = jax.random.split(key)
    row_level = jnp.arange(DOUT, dtype=jnp.float32) / DOUT
    entries = jnp.exp(jax.random.uniform(key_entry, (DOUT, DIN), jnp.float32, jnp.log(0.5), jnp.log(2.0)))
    column_level = jax.random.uniform(key_column, (DIN,), jnp.float32, 0.0, 1.0)
    values = jnp.power(10.0, row_level)[:, None] * jnp.power(10.0, column_level)[None, :] * entries
    return jnp.clip(values, 0.5, 199.0).astype(jnp.bfloat16)


def shard_levels(rng, extent, pieces, low, top_value):
    def one(axis_at, parts):
        steps = jax.random.uniform(jax.random.fold_in(jax.random.fold_in(rng, 6), axis_at), (parts,), jnp.float32, low / len(pieces), top_value / len(pieces))
        return jnp.repeat(jnp.exp(steps), extent[axis_at] // parts).reshape((-1,) + (1,) * (len(extent) - axis_at - 1))

    factor_of = one(*pieces[0])
    for cut in pieces[1:]:
        factor_of = factor_of * one(*cut)
    return factor_of


def gaussian(own_key, extent, scale, bound, cuts=(), kind=jnp.bfloat16):
    result = jax.random.normal(own_key, extent, jnp.float32) * scale
    if len(cuts) > 0:
        result = shard_levels(own_key, extent, cuts, -0.22, 0.18) * result
    return jnp.clip(result, min=-bound, max=bound).astype(kind)


def setup_inputs(seed: int = 0) -> dict:
    streams_of = jax.random.split(jax.random.key(seed), 8)
    return {
        "grads_out": gaussian(streams_of[0], (POOL, DOUT), 1.0, 6.0, ((0, 32), (1, 16))),
        "acts": gaussian(streams_of[1], (POOL, DIN), 1.0, 6.0, ((0, 16), (1, 32))),
        "query_index": draw_query_index(jax.random.fold_in(streams_of[7], 71), 0),
        "train_index": draw_train_index(jax.random.fold_in(streams_of[7], 71), 0),
        "out_basis": gaussian(streams_of[4], (DOUT, DOUT), DOUT ** -0.5, 0.03125, ((0, 16), (1, 32))),
        "in_basis": gaussian(streams_of[5], (DIN, DIN), DIN ** -0.5, 0.0625, ((0, 32), (1, 16))),
        "eig_products": draw_eig_products(jax.random.fold_in(streams_of[7], 71), 0),
    }


def reference(grads_out, acts, query_index, train_index, out_basis, in_basis, eig_products):
    picked = jnp.concatenate([query_index, train_index]).astype(jnp.int32)
    grad_rows = jnp.take(grads_out, picked, axis=0)
    act_rows = jnp.take(acts, picked, axis=0)
    rot_out = jnp.dot(grad_rows, out_basis, preferred_element_type=jnp.float32).astype(jnp.bfloat16)
    rot_in = jnp.dot(act_rows, in_basis, preferred_element_type=jnp.float32).astype(jnp.bfloat16)
    damping = 0.1 * jnp.sum(eig_products.astype(jnp.float32)) / (DOUT * DIN)
    query_count = query_index.shape[0]
    query_out = rot_out[:query_count].astype(jnp.float32)
    train_out = rot_out[query_count:].astype(jnp.float32)
    query_in = rot_in[:query_count].astype(jnp.float32)
    train_in = rot_in[query_count:].astype(jnp.float32)
    block_rows = DOUT // N_ROW

    def one_block(totals, begin):
        eig_rows = lax.dynamic_slice_in_dim(eig_products, begin, block_rows, 0).astype(jnp.float32)
        inverse = 1.0 / (eig_rows + damping)
        query_part = lax.dynamic_slice_in_dim(query_out, begin, block_rows, 1)
        train_part = lax.dynamic_slice_in_dim(train_out, begin, block_rows, 1)
        precond = (query_part[:, :, None] * query_in[:, None, :] * inverse[None]).astype(jnp.bfloat16)
        precond = lax.optimization_barrier(precond).astype(jnp.float32)
        mixed = jnp.einsum('ti,qij->qtj', train_part, precond)
        return (totals + lax.optimization_barrier(jnp.sum(mixed * train_in[None], axis=2)), None)
    begins = (jnp.arange(N_ROW) * block_rows).astype(jnp.int32)
    zeros_init = jnp.zeros((query_count, train_index.shape[0]), jnp.float32)
    totals, _ = lax.scan(one_block, zeros_init, begins)
    return totals * (1.0 / math.sqrt(DOUT * DIN))
```

```python
import math

import jax
import jax.numpy as jnp
from jax import lax
from jax.experimental import pallas as pl
from jax.experimental.pallas import tpu as pltpu
from jax.sharding import PartitionSpec as P

DOUT = 28672
DIN = 8192
QUERIES = 8
TRAIN = 384
POOL = 1024
X, Y, Z = 4, 8, 8
PICKS = 400
CA = 768
CB = 1024
IB = 896
JB = 512
TCH = 48
CH = 56
MESH = pl.DeviceIdType.MESH
F32 = jnp.float32
BF16 = jnp.bfloat16
PARTS = ((0, 24), (24, 32))
N_SEM = 144


def kernel(
    wanted, grads, acts, out_basis, in_basis, eig, out,
    pool_a, pool_b, pool_c, hot_a, hot_b, hot_c, obv, ibv, eigv, inverse, picked,
    part, swap, ringbuf, sendbuf, own, own_other, rout, rquery,
    in_part, in_x, in_sum, in_y, rin, damp_s, damp_z, damp_y, damp_x,
    fin_s, fin_z, fin_y, fin_x, send_sems, recv_sems, load_sems,
):
    row = lax.axis_index("row")
    col = lax.axis_index("col")
    x, y = row // Y, row % Y
    z, k = col // 2, col % 2
    other = 1 - k
    turn = 1 - 2 * k

    def dev(ox=0, oy=0, oz=0):
        return (((x + ox + X) % X) * Y + (y + oy + Y) % Y, ((z + oz + Z) % Z) * 2 + k)

    sibling = (row, z * 2 + other)
    used = [0]
    pending = []

    def remote(src, dst, target, start=True):
        at = used[0]
        used[0] += 1
        copy = pltpu.make_async_remote_copy(
            src_ref=src, dst_ref=dst, send_sem=send_sems.at[at], recv_sem=recv_sems.at[at],
            device_id=target, device_id_type=MESH,
        )
        if start:
            copy.start()
            pending.append(copy)
        return copy

    def rows(start, size):
        return pl.ds(pl.multiple_of(start, 8), size)

    def at_a(px, py):
        return pl.ds(pl.multiple_of(((py + Y) % Y) * 128 + ((px + X) % X) * 32, 32), 32)

    def at_b(px, py, size=32, skip=0):
        return pl.ds(pl.multiple_of(((px + X) % X) * 256 + ((py + Y) % Y) * 32 + skip, 16), size)

    def at_a_group(py, size=128, skip=0):
        return pl.ds(pl.multiple_of(((py + Y) % Y) * 128 + skip, 32), size)

    own_c = pl.ds(pl.multiple_of(k * 512 + z * 64, 64), 64)
    loads = [
        pltpu.make_async_copy(grads.at[:, pl.ds(CA, CB)], pool_b.at[at_b(x, y)], load_sems.at[0]),
        pltpu.make_async_copy(grads.at[:, pl.ds(0, CA)], pool_a.at[at_a(x, y)], load_sems.at[1]),
        pltpu.make_async_copy(acts, pool_c.at[own_c], load_sems.at[2]),
        pltpu.make_async_copy(eig, eigv, load_sems.at[3]),
        pltpu.make_async_copy(in_basis, ibv, load_sems.at[4]),
        pltpu.make_async_copy(out_basis, obv, load_sems.at[5]),
    ]
    for load in loads:
        load.start()

    @pl.when(k == 1)
    def _():
        ringbuf[0] = jnp.zeros((CH, IB), F32)

    barrier = pltpu.get_barrier_semaphore()
    partners = [sibling]
    partners += [dev(oz=o) for o in range(1, Z)]
    partners += [dev(oy=o) for o in range(1, Y)]
    partners += [dev(ox=o) for o in range(1, X)]
    for partner in partners:
        pl.semaphore_signal(barrier, inc=1, device_id=partner, device_id_type=MESH)
    for load in loads[:3]:
        load.wait()
    pl.semaphore_wait(barrier, len(partners))

    def go(buf, where, **to):
        return remote(buf.at[where], buf.at[where], dev(**to))

    b_y = {}
    b_x = {}
    b_x2 = {}
    a_y = {}
    b_y[1] = [go(pool_b, at_b(x, y), oy=1), go(pool_b, at_b(x, y), oy=-1)]
    a_x = [go(pool_a, at_a(x, y), ox=o) for o in (1, 3, 2)]
    b_x[0] = [go(pool_b, at_b(x, y), ox=1), go(pool_b, at_b(x, y), ox=-1)]
    a_y[1] = [go(pool_a, at_a(x, y), oy=1), go(pool_a, at_a(x, y), oy=-1)]
    c_z = [go(pool_c, own_c, oz=o) for o in (1, 7, 2, 6, 3, 5, 4)]

    loads[3].wait()
    total = jnp.zeros((8, 128), F32)
    for at in range(0, IB, 128):
        block = eigv[at:at + 128, :].astype(F32)
        for at_lane in range(0, JB, 128):
            total = total + jnp.sum(block[:, at_lane:at_lane + 128].reshape(16, 8, 128), axis=0)

    def sum_start(buf, me, value, targets):
        buf[me] = value
        return [remote(buf.at[me], buf.at[me], target) for target in targets]

    def sum_end(buf, copies):
        for copy in copies:
            copy.wait_recv()
        result = buf[0]
        for at in range(1, buf.shape[0]):
            result = result + buf[at]
        return result

    to_z = [dev(oz=o) for o in range(1, Z)]
    to_y = [dev(oy=o) for o in range(1, Y)]
    to_x = [dev(ox=o) for o in range(1, X)]
    damp = sum_start(damp_s, k, total, [sibling])

    want = wanted[...]
    place = lax.broadcasted_iota(jnp.int32, (PICKS, POOL), 1)
    hot_b[...] = (place == want).astype(F32).astype(BF16)
    hot_a[...] = (((place // 32) % 4) * 256 + (place // 128) * 32 + place % 32 == want).astype(F32).astype(BF16)
    hot_c[...] = (((place // 64) % 8) * 128 + (place // 512) * 64 + place % 64 == want).astype(F32).astype(BF16)

    for copy in b_y[1]:
        copy.wait_recv()
    b_y[2] = [go(pool_b, at_b(x, y - 1), oy=1), go(pool_b, at_b(x, y + 1), oy=-1)]
    for j in (-1, 1):
        b_x[j] = [go(pool_b, at_b(x, y + j), ox=1), go(pool_b, at_b(x, y + j), ox=-1)]
    for o, copy in zip((1, 3, 2), a_x):
        copy.wait_recv()
        a_y[1] += [go(pool_a, at_a(x - o, y), oy=1), go(pool_a, at_a(x - o, y), oy=-1)]
    damp = sum_start(damp_z, z, sum_end(damp_s, damp), to_z)

    for copy in b_y[2]:
        copy.wait_recv()
    b_y[3] = [go(pool_b, at_b(x, y - 2), oy=1), go(pool_b, at_b(x, y + 2), oy=-1)]
    for j in (-2, 2):
        b_x[j] = [go(pool_b, at_b(x, y + j), ox=1), go(pool_b, at_b(x, y + j), ox=-1)]
    for copy in a_y[1]:
        copy.wait_recv()
    a_y[2] = [go(pool_a, at_a_group(y - 1), oy=1), go(pool_a, at_a_group(y + 1), oy=-1)]

    def b_cross(j):
        for copy in b_x[j]:
            copy.wait_recv()
        if j in (0, 1, 2, 3):
            b_x2[j] = go(pool_b, at_b(x - 1, y + j), ox=1)
        else:
            b_x2[j] = go(pool_b, at_b(x + 1, y + j), ox=-1)

    b_cross(0)
    for copy in c_z:
        copy.wait_recv()
    half_c = pl.ds(pl.multiple_of(k * 512, 512), 512)
    c_s = remote(pool_c.at[half_c], pool_c.at[half_c], sibling)
    damp = sum_start(damp_y, y, sum_end(damp_z, damp), to_y)

    for copy in b_y[3]:
        copy.wait_recv()
    b_y[4] = [
        remote(pool_b.at[at_b(x, y - 3, 16)], pool_b.at[at_b(x, y - 3, 16)], dev(oy=1)),
        remote(pool_b.at[at_b(x, y + 3, 16, 16)], pool_b.at[at_b(x, y + 3, 16, 16)], dev(oy=-1)),
    ]
    for j in (-3, 3):
        b_x[j] = [go(pool_b, at_b(x, y + j), ox=1), go(pool_b, at_b(x, y + j), ox=-1)]
    for copy in a_y[2]:
        copy.wait_recv()
    a_y[3] = [go(pool_a, at_a_group(y - 2), oy=1), go(pool_a, at_a_group(y + 2), oy=-1)]
    b_cross(1)
    b_cross(-1)

    c_s.wait_recv()
    loads[4].wait()
    act_rows = jnp.dot(hot_c[...], pool_c[...], preferred_element_type=F32).astype(BF16)
    for at in range(X):
        in_part[at] = jnp.dot(act_rows, ibv[:, at * 128:at * 128 + 128], preferred_element_type=F32)

    for copy in b_y[4]:
        copy.wait_recv()
    b_x[4] = [go(pool_b, at_b(x, y + 4), ox=1), go(pool_b, at_b(x, y + 4), ox=-1)]
    for copy in a_y[3]:
        copy.wait_recv()
    a_y[4] = [
        go(pool_a, at_a_group(y - 3, 64), oy=1),
        go(pool_a, at_a_group(y + 3, 64, 64), oy=-1),
    ]
    for j in (2, -2, 3, -3, 4):
        b_cross(j)
    damp = sum_start(damp_x, x, sum_end(damp_y, damp), to_x)

    in_copies = [
        remote(in_part.at[(x + o) % X], in_x.at[o - 1], dev(ox=o)) for o in range(1, X)
    ]

    for copy in a_y[4]:
        copy.wait_recv()
    for at in range(0, CA, 256):
        picked[:, at:at + 256] = jnp.dot(
            hot_a[...], pool_a[:, at:at + 256], preferred_element_type=F32
        ).astype(BF16)
    for j in b_x2:
        b_x2[j].wait_recv()
    for at in range(0, CB, 256):
        picked[:, CA + at:CA + at + 256] = jnp.dot(
            hot_b[...], pool_b[:, at:at + 256], preferred_element_type=F32
        ).astype(BF16)
    loads[5].wait()
    for at in range(0, IB, 256):
        width = min(256, IB - at)
        rotated = jnp.dot(picked[...], obv[:, at:at + width], preferred_element_type=F32)
        for d in range(Z):
            part[d * CH:d * CH + TCH, at:at + width] = rotated[d * TCH:d * TCH + TCH]
            part[d * CH + TCH:d * CH + CH, at:at + width] = rotated[TRAIN:TRAIN + QUERIES]

    def chunk(d):
        return rows(((d + 2 * Z) % Z) * CH, CH)

    swaps = []
    for j in range(4):
        need = jnp.where(k == 1, z + 4 - j, z if j == 0 else z - 4 + j)
        swaps.append(remote(part.at[chunk(need)], swap.at[j], sibling))

    hops = []
    for s in range(4):
        swaps[s].wait_recv()
        mine = part.at[chunk(z + turn * (4 - s))]
        hop = []
        for p, (first, size) in enumerate(PARTS):
            span = pl.ds(first, size)
            if s > 0:
                if s == 1:
                    @pl.when(k == 0)
                    def _():
                        hops[0][p].wait_recv()
                else:
                    hops[s - 1][p].wait_recv()
                sendbuf[s, span] = mine[span] + swap[s, span] + ringbuf[s - 1, span]
            else:
                sendbuf[s, span] = mine[span] + swap[s, span]
            copy = remote(
                sendbuf.at[s, span], ringbuf.at[s, span], dev(oz=turn), start=s > 0
            )
            if s == 0:
                @pl.when(k == 0)
                def _():
                    copy.start()
            hop.append(copy)
        hops.append(hop)
        if s == 1:
            for copy in in_copies:
                copy.wait_recv()
            sums = in_part[x]
            for o in range(1, X):
                sums = sums + in_x[o - 1]
            for d in range(Y):
                in_sum[d, 0:TCH] = sums[d * TCH:d * TCH + TCH]
                in_sum[d, TCH:CH] = sums[TRAIN:TRAIN + QUERIES]
            in_copies = [
                remote(in_sum.at[(y + o) % Y], in_y.at[o - 1], dev(oy=o)) for o in range(1, Y)
            ]
        if s == 2:
            damping = 0.1 * jnp.sum(sum_end(damp_x, damp)) / (DOUT * DIN)
            inverse[...] = 1.0 / (eigv[...].astype(F32) + damping)

    def in_middle():
        for copy in in_copies:
            copy.wait_recv()
        sums = in_sum[y]
        for o in range(1, Y):
            sums = sums + in_y[o - 1]
        rin[x, pl.ds(pl.multiple_of(y * TCH, 16), TCH)] = sums[0:TCH].astype(BF16)
        rin[x, TRAIN:PICKS] = jnp.concatenate([sums[TCH:CH], sums[TCH:CH]], axis=0).astype(BF16)
        span = pl.ds(pl.multiple_of(y * TCH, 16), TCH)
        return [remote(rin.at[x, span], rin.at[x, span], dev(oy=o)) for o in range(1, Y)]

    for p, (first, size) in enumerate(PARTS):
        span = pl.ds(first, size)
        hops[3][p].wait_recv()
        rest = part[rows(z * CH + first, size)] + swap[0, span]
        own[span] = ringbuf[3, span] + jnp.where(k == 1, rest, 0.0)
    meet = remote(own, own_other, sibling)
    in_copies = in_middle()
    meet.wait_recv()
    full = own[...] + own_other[...]
    rquery[...] = full[TCH:CH].astype(BF16).astype(F32)
    mine = pl.ds(pl.multiple_of(z * TCH, 16), TCH)
    rout[mine] = full[0:TCH].astype(BF16)

    spread = []
    for o in (4, 1, 2, 3):
        copy = remote(rout.at[mine], rout.at[mine], dev(oz=turn * o), start=o < 4)
        if o == 4:
            @pl.when(k == 0)
            def _():
                copy.start()
        spread.append((o, copy))

    for copy in in_copies:
        copy.wait_recv()
    in_copies = [remote(rin.at[x], rin.at[x], dev(ox=o)) for o in range(1, X)]

    across = []
    for o, copy in spread[1:] + spread[:1]:
        span = pl.ds(pl.multiple_of(((z - turn * o + Z) % Z) * TCH, 16), TCH)
        relay = remote(rout.at[span], rout.at[span], sibling, start=False)
        if o < 4:
            copy.wait_recv()
            relay.start()
            pending.append(relay)
        else:
            @pl.when(k == 0)
            def _():
                copy.wait_recv()
                relay.start()
        across.append((o, copy, relay))
    for copy in in_copies:
        copy.wait_recv()
    for o, copy, relay in across:
        if o < 4:
            relay.wait_recv()
        else:
            @pl.when(k == 1)
            def _():
                relay.wait_recv()

    query_columns = jnp.transpose(rquery[...])
    lanes = lax.broadcasted_iota(jnp.int32, (TRAIN, 128), 1)
    collected = jnp.zeros((TRAIN, 128), F32)
    for q in range(QUERIES):
        column = query_columns[:, q:q + 1]
        total = jnp.zeros((TRAIN, 128), F32)
        for at in range(0, X, 2):
            halves = []
            for t in (at, at + 1):
                line = rin[t, TRAIN:PICKS].astype(F32)[q:q + 1]
                halves.append((column * line * inverse[:, t * 128:t * 128 + 128]).astype(BF16))
            mixed = jnp.dot(rout[...], jnp.concatenate(halves, axis=1), preferred_element_type=F32)
            for n, t in enumerate((at, at + 1)):
                total = total + mixed[:, n * 128:n * 128 + 128] * rin[t, 0:TRAIN].astype(F32)
        collected = jnp.where(lanes == q, jnp.sum(total, axis=1, keepdims=True), collected)
    scores = jnp.transpose(collected)[0:QUERIES]

    fin = sum_start(fin_s, k, scores, [sibling])
    fin = sum_start(fin_z, z, sum_end(fin_s, fin), to_z)
    fin = sum_start(fin_y, y, sum_end(fin_z, fin), to_y)
    fin = sum_start(fin_x, x, sum_end(fin_y, fin), to_x)
    out[...] = sum_end(fin_x, fin) * (1.0 / math.sqrt(DOUT * DIN))

    for copy in pending:
        copy.wait_send()

    @pl.when(k == 0)
    def _():
        for copy in hops[0] + [spread[0][1], across[-1][2]]:
            copy.wait_send()


def per_device(grads_out, acts, query_index, train_index, out_basis, in_basis, eig_products):
    padding = jnp.full((PICKS - TRAIN - QUERIES,), -1, jnp.int32)
    wanted = jnp.concatenate([train_index, query_index, padding])[:, None]
    vmem = pl.BlockSpec(memory_space=pltpu.VMEM)
    hbm = pl.BlockSpec(memory_space=pl.ANY)
    return pl.pallas_call(
        kernel,
        out_shape=jax.ShapeDtypeStruct((QUERIES, TRAIN), F32),
        in_specs=[vmem] + [hbm] * 5,
        out_specs=vmem,
        scratch_shapes=[
            pltpu.VMEM((POOL, CA), BF16),
            pltpu.VMEM((POOL, CB), BF16),
            pltpu.VMEM((POOL, 256), BF16),
            pltpu.VMEM((PICKS, POOL), BF16),
            pltpu.VMEM((PICKS, POOL), BF16),
            pltpu.VMEM((PICKS, POOL), BF16),
            pltpu.VMEM((CA + CB, IB), BF16),
            pltpu.VMEM((256, JB), BF16),
            pltpu.VMEM((IB, JB), BF16),
            pltpu.VMEM((IB, JB), F32),
            pltpu.VMEM((PICKS, CA + CB), BF16),
            pltpu.VMEM((Z * CH, IB), F32),
            pltpu.VMEM((4, CH, IB), F32),
            pltpu.VMEM((4, CH, IB), F32),
            pltpu.VMEM((4, CH, IB), F32),
            pltpu.VMEM((CH, IB), F32),
            pltpu.VMEM((CH, IB), F32),
            pltpu.VMEM((TRAIN, IB), BF16),
            pltpu.VMEM((QUERIES, IB), F32),
            pltpu.VMEM((X, PICKS, 128), F32),
            pltpu.VMEM((X - 1, PICKS, 128), F32),
            pltpu.VMEM((Y, CH, 128), F32),
            pltpu.VMEM((Y - 1, CH, 128), F32),
            pltpu.VMEM((X, PICKS, 128), BF16),
            pltpu.VMEM((2, 8, 128), F32),
            pltpu.VMEM((Z, 8, 128), F32),
            pltpu.VMEM((Y, 8, 128), F32),
            pltpu.VMEM((X, 8, 128), F32),
            pltpu.VMEM((2, QUERIES, TRAIN), F32),
            pltpu.VMEM((Z, QUERIES, TRAIN), F32),
            pltpu.VMEM((Y, QUERIES, TRAIN), F32),
            pltpu.VMEM((X, QUERIES, TRAIN), F32),
            pltpu.SemaphoreType.DMA((N_SEM,)),
            pltpu.SemaphoreType.DMA((N_SEM,)),
            pltpu.SemaphoreType.DMA((6,)),
        ],
        compiler_params=pltpu.CompilerParams(
            collective_id=0, has_side_effects=True, vmem_limit_bytes=56 * 2**20
        ),
    )(wanted, grads_out, acts, out_basis, in_basis, eig_products)


def solution(mesh):
    in_specs = (
        P("row", "col"),
        P("col", "row"),
        P(),
        P(),
        P("col", "row"),
        P("row", "col"),
        P("row", "col"),
    )
    return jax.shard_map(
        per_device, mesh=mesh, in_specs=in_specs, out_specs=P(), check_vma=False
    )
```

```python
import math

import jax
import jax.numpy as jnp
from jax import lax
from jax.experimental import pallas as pl
from jax.experimental.pallas import tpu as pltpu
from jax.sharding import PartitionSpec as P

DOUT = 28672
DIN = 8192
QUERIES = 8
TRAIN = 384
POOL = 1024
X, Y, Z = 4, 8, 8
PICKS = 400
CA = 768
CB = 1024
IB = 896
JB = 512
TCH = 48
CH = 56
MESH = pl.DeviceIdType.MESH
F32 = jnp.float32
BF16 = jnp.bfloat16
PARTS = ((0, 16), (16, 16), (32, 24))
N_SEM = 208
ORDER = (
    ('A', 0, 1), ('A', 0, 3), ('B', 1), ('B', -1), ('Bx', 0, -1), ('eig',), ('A', 0, 2), ('Bx', 0, 1),
    ('B', 2), ('B', -2), ('A', 1, 0), ('A', -1, 0), ('damp_z',), ('A', 1, 1), ('A', -1, 1), ('Bx', 1, 1),
    ('Bx', 1, -1), ('A', 1, 3), ('A', -1, 3), ('hot_c',), ('Bx', -1, 1), ('Bx', -1, -1), ('hot_b',),
    ('A', 1, 2), ('A', -1, 2), ('Bxx', 0), ('acts',), ('Bx', 2, -1), ('B', 3), ('B', -3), ('Bx', 2, 1),
    ('Bx', -2, -1), ('damp_y',), ('B', 4), ('B', -4), ('Bx', -2, 1), ('A', 2, 0), ('A', -2, 0), ('A', 2, 1),
    ('A', -2, 1), ('Bxx', 1), ('in_rot',), ('Bxx', -1), ('A', 2, 3), ('A', -2, 3), ('A', 2, 2), ('A', -2, 2),
    ('hot_a',), ('Bx', 3, 1), ('pick_b', 0), ('Bx', 3, -1), ('Bx', -3, 1), ('Bx', -3, -1), ('A', 3, 0),
    ('A', -3, 0), ('Bxx', 2), ('Bxx', -2), ('A', 3, 1), ('A', -3, 1), ('Bx', 4, 1), ('Bx', 4, -1),
    ('damp_x',), ('A', 3, 3), ('Bx', -4, 1), ('Bx', -4, -1), ('pick_b', 1), ('pick_b', 3), ('A', -3, 3),
    ('A', 3, 2), ('A', -3, 2), ('Bxx', 3), ('in_x',), ('A', 4, 0), ('A', -4, 0), ('Bxx', -3), ('A', 4, 1),
    ('A', -4, 1), ('Bxx', 4), ('A', 4, 3), ('A', -4, 3), ('Bxx', -4), ('A', 4, 2), ('A', -4, 2),
)


def kernel(
    train_index, query_index, grads, acts, out_basis, in_basis, eig, out,
    want_rows, pool_a, pool_b, pool_c, sum_b, hot_a, hot_b, hot_c, obv, ibv, eigv, inverse, picked,
    part, swap, ringbuf, sendbuf, own, own_other, rout, rquery,
    in_part, in_relay, in_send, in_x, in_sum, in_y, rin, rin_query, precond, damp_s, damp_z, damp_y, damp_x,
    fin_s, fin_z, fin_y, fin_x, send_sems, recv_sems, load_sems,
):
    row = lax.axis_index("row")
    col = lax.axis_index("col")
    x, y = row // Y, row % Y
    z, k = col // 2, col % 2
    other = 1 - k
    turn = 1 - 2 * k

    def dev(ox=0, oy=0, oz=0):
        return (((x + ox + X) % X) * Y + (y + oy + Y) % Y, ((z + oz + Z) % Z) * 2 + k)

    sibling = (row, z * 2 + other)
    used = [0]
    pending = []

    def remote(src, dst, target, start=True):
        at = used[0]
        used[0] += 1
        copy = pltpu.make_async_remote_copy(
            src_ref=src, dst_ref=dst, send_sem=send_sems.at[at], recv_sem=recv_sems.at[at],
            device_id=target, device_id_type=MESH,
        )
        if start:
            copy.start()
            pending.append(copy)
        return copy

    def rows(start, size):
        return pl.ds(pl.multiple_of(start, 8), size)

    barrier = pltpu.get_barrier_semaphore()
    partners = [sibling]
    partners += [dev(oz=o) for o in range(1, Z)]
    partners += [dev(oy=o) for o in range(1, Y)]
    partners += [dev(ox=o) for o in range(1, X)]
    for partner in partners:
        pl.semaphore_signal(barrier, inc=1, device_id=partner, device_id_type=MESH)

    def at_a(px, py):
        return pl.ds(pl.multiple_of(((py + Y) % Y) * 128 + ((px + X) % X) * 32, 32), 32)

    def at_b(px, py, size=32, skip=0):
        return pl.ds(pl.multiple_of(((px + X) % X) * 256 + ((py + Y) % Y) * 32 + skip, 16), size)

    own_c = pl.ds(pl.multiple_of(k * 512 + z * 64, 64), 64)
    loads = [
        pltpu.make_async_copy(grads.at[:, pl.ds(CA, CB)], pool_b.at[at_b(x, y)], load_sems.at[0]),
        pltpu.make_async_copy(grads.at[:, pl.ds(0, CA)], pool_a.at[at_a(x, y)], load_sems.at[1]),
        pltpu.make_async_copy(acts, pool_c.at[own_c], load_sems.at[2]),
        pltpu.make_async_copy(eig, eigv, load_sems.at[3]),
        pltpu.make_async_copy(in_basis, ibv, load_sems.at[4]),
        pltpu.make_async_copy(out_basis, obv, load_sems.at[5]),
    ]
    for load in loads[:4]:
        load.start()

    @pl.when(k == 1)
    def _():
        ringbuf[0] = jnp.zeros((CH, IB), F32)

    for load in loads[:3]:
        load.wait()
    pl.semaphore_wait(barrier, len(partners))

    coming = {}

    def go(event, buf, where, **to):
        coming[event] = remote(buf.at[where], buf.at[where], dev(**to))

    def block_b(px, d):
        if abs(d) == 4:
            return at_b(px, y - 4, 16, 0 if d > 0 else 16)
        return at_b(px, y - d)

    def on_b(d):
        if abs(d) == 2:
            s = d // 2
            go(("B", 3 * s), pool_b, at_b(x, y - d), oy=s)
            go(("B", 4 * s), pool_b, at_b(x, y - d, 16, 0 if s > 0 else 16), oy=2 * s)
        go(("Bx", d, 1), pool_b, block_b(x, d), ox=1)
        go(("Bx", d, -1), pool_b, block_b(x, d), ox=-1)

    def on_bx(d, s):
        if (s > 0) == (d in (0, 1, 2, 3)):
            go(("Bxx", d), pool_b, block_b(x - s, d), ox=s)

    def on_a(d, o):
        where = at_a(x - o, y - d)
        if d == 0:
            go(("A", 1, o), pool_a, where, oy=1)
            go(("A", -1, o), pool_a, where, oy=-1)
        elif abs(d) < 3:
            s = 1 if d > 0 else -1
            go(("A", d + s, o), pool_a, where, oy=s)
        elif abs(d) == 3 and (d > 0) == (o < 2):
            s = d // 3
            go(("A", 4 * s, o), pool_a, where, oy=s)

    go(("B", 1), pool_b, at_b(x, y), oy=1)
    go(("B", -1), pool_b, at_b(x, y), oy=-1)
    for o in (1, 3, 2):
        go(("A", 0, o), pool_a, at_a(x, y), ox=o)
    go(("B", 2), pool_b, at_b(x, y), oy=2)
    go(("B", -2), pool_b, at_b(x, y), oy=-2)
    on_a(0, 0)
    go(("Bx", 0, 1), pool_b, at_b(x, y), ox=1)
    go(("Bx", 0, -1), pool_b, at_b(x, y), ox=-1)
    c_z = [remote(pool_c.at[own_c], pool_c.at[own_c], dev(oz=o)) for o in (1, 7, 2, 6, 3, 5, 4)]
    for load in loads[4:]:
        load.start()

    def sum_start(buf, me, value, targets):
        buf[me] = value
        return [remote(buf.at[me], buf.at[me], target) for target in targets]

    def sum_end(buf, copies):
        for copy in copies:
            copy.wait_recv()
        result = buf[0]
        for at in range(1, buf.shape[0]):
            result = result + buf[at]
        return result

    to_z = [dev(oz=o) for o in range(1, Z)]
    to_y = [dev(oy=o) for o in range(1, Y)]
    to_x = [dev(ox=o) for o in range(1, X)]

    train_line = jnp.broadcast_to(train_index[...].reshape(1, TRAIN).astype(F32), (8, TRAIN))
    want_rows[0:TRAIN] = jnp.transpose(train_line)[:, 0:1].astype(jnp.int32)
    lines = lax.broadcasted_iota(jnp.int32, (PICKS - TRAIN, 1), 0)
    query_rows = jnp.full((PICKS - TRAIN, 1), -1, jnp.int32)
    for q in range(QUERIES):
        query_rows = jnp.where(lines == q, query_index[q], query_rows)
    want_rows[TRAIN:PICKS] = query_rows

    def mark(hot, order):
        place = lax.broadcasted_iota(jnp.int32, (PICKS, POOL), 1)
        hot[...] = (order(place) == want_rows[...]).astype(F32).astype(BF16)

    def pick_b(o, last=False):
        group = pl.ds(pl.multiple_of(((x + X - o) % X) * 256, 256), 256)
        for at in range(0, CB, 256):
            some = jnp.dot(hot_b[:, group], pool_b[group, at:at + 256], preferred_element_type=F32)
            if o > 0:
                some = some + sum_b[:, at:at + 256]
            if last:
                picked[:, CA + at:CA + at + 256] = some.astype(BF16)
            else:
                sum_b[:, at:at + 256] = some

    half = PICKS // 2
    low, high = pl.ds(0, half), pl.ds(half, half)
    right, left, across = (x + 1) % X, (x + 3) % X, (x + 2) % X
    for event in ORDER:
        if event in coming:
            coming[event].wait_recv()
        kind = event[0]
        if kind == "A":
            on_a(*event[1:])
        elif kind == "B":
            on_b(*event[1:])
        elif kind == "Bx":
            on_bx(*event[1:])
        elif kind == "eig":
            loads[3].wait()
            total = jnp.zeros((8, 128), F32)
            for at in range(0, IB, 128):
                block = eigv[at:at + 128, :].astype(F32)
                for at_lane in range(0, JB, 128):
                    total = total + jnp.sum(block[:, at_lane:at_lane + 128].reshape(16, 8, 128), axis=0)
            damp = sum_start(damp_s, k, total, [sibling])
        elif kind == "hot_a":
            mark(hot_a, lambda at: ((at // 32) % 4) * 256 + (at // 128) * 32 + at % 32)
        elif kind == "hot_b":
            mark(hot_b, lambda at: at)
        elif kind == "hot_c":
            mark(hot_c, lambda at: ((at // 64) % 8) * 128 + (at // 512) * 64 + at % 64)
        elif kind == "pick_b":
            pick_b(event[1])
        elif kind == "damp_z":
            damp = sum_start(damp_z, z, sum_end(damp_s, damp), to_z)
        elif kind == "damp_y":
            damp = sum_start(damp_y, y, sum_end(damp_z, damp), to_y)
        elif kind == "damp_x":
            damp = sum_start(damp_x, x, sum_end(damp_y, damp), to_x)
        elif kind == "acts":
            for copy in c_z:
                copy.wait_recv()
            half_c = pl.ds(pl.multiple_of(k * 512, 512), 512)
            c_s = remote(pool_c.at[half_c], pool_c.at[half_c], sibling)
        elif kind == "in_rot":
            c_s.wait_recv()
            loads[4].wait()
            act_rows = jnp.dot(hot_c[...], pool_c[...], preferred_element_type=F32).astype(BF16)
            for at in range(X):
                in_part[at] = jnp.dot(
                    act_rows, ibv[:, at * 128:at * 128 + 128], preferred_element_type=F32
                )
        elif kind == "in_x":
            relays = [
                remote(in_part.at[across, low], in_relay.at[0], dev(ox=1)),
                remote(in_part.at[across, high], in_relay.at[1], dev(ox=-1)),
            ]
            in_copies = [
                remote(in_part.at[right, high], in_x.at[0, high], dev(ox=1)),
                remote(in_part.at[left, low], in_x.at[1, low], dev(ox=-1)),
            ]

    for at in range(0, CA, 256):
        picked[:, at:at + 256] = jnp.dot(
            hot_a[...], pool_a[:, at:at + 256], preferred_element_type=F32
        ).astype(BF16)
    pick_b(2, last=True)
    for copy in relays:
        copy.wait_recv()
    in_send[0] = in_relay[0] + in_part[right, low]
    in_send[1] = in_relay[1] + in_part[left, high]
    in_copies += [
        remote(in_send.at[0], in_x.at[0, low], dev(ox=1)),
        remote(in_send.at[1], in_x.at[1, high], dev(ox=-1)),
    ]

    def chunk(d):
        return rows(((d + 2 * Z) % Z) * CH, CH)

    loads[5].wait()
    swaps = [[] for _ in range(4)]
    for start, end in ((0, 512), (512, IB)):
        for at in range(start, end, 256):
            width = min(256, IB - at)
            rotated = jnp.dot(picked[...], obv[:, at:at + width], preferred_element_type=F32)
            for d in range(Z):
                part[d * CH:d * CH + TCH, at:at + width] = rotated[d * TCH:d * TCH + TCH]
                part[d * CH + TCH:d * CH + CH, at:at + width] = rotated[TRAIN:TRAIN + QUERIES]
        span = pl.ds(start, end - start)
        for j in range(4):
            need = jnp.where(k == 1, z + 4 - j, z if j == 0 else z - 4 + j)
            swaps[j].append(remote(part.at[chunk(need), span], swap.at[j, :, span], sibling))

    hops = []
    for s in range(4):
        for copy in swaps[s]:
            copy.wait_recv()
        mine = part.at[chunk(z + turn * (4 - s))]
        hop = []
        for p, (first, size) in enumerate(PARTS):
            span = pl.ds(first, size)
            if s > 0:
                if s == 1:
                    @pl.when(k == 0)
                    def _():
                        hops[0][p].wait_recv()
                else:
                    hops[s - 1][p].wait_recv()
                sendbuf[s, span] = mine[span] + swap[s, span] + ringbuf[s - 1, span]
            else:
                sendbuf[s, span] = mine[span] + swap[s, span]
            copy = remote(
                sendbuf.at[s, span], ringbuf.at[s, span], dev(oz=turn), start=s > 0
            )
            if s == 0:
                @pl.when(k == 0)
                def _():
                    copy.start()
            hop.append(copy)
        hops.append(hop)
        if s == 0:
            for copy in in_copies:
                copy.wait_recv()
            sums = in_part[x] + in_x[0] + in_x[1]
            for d in range(Y):
                in_sum[d, 0:TCH] = sums[d * TCH:d * TCH + TCH]
                in_sum[d, TCH:CH] = sums[TRAIN:TRAIN + QUERIES]
            in_copies = [
                remote(in_sum.at[(y + o) % Y], in_y.at[o - 1], dev(oy=o)) for o in range(1, Y)
            ]
        if s == 2:
            damping = 0.1 * jnp.sum(sum_end(damp_x, damp)) / (DOUT * DIN)
            inverse[...] = 1.0 / (eigv[...].astype(F32) + damping)

    def in_middle():
        for copy in in_copies:
            copy.wait_recv()
        sums = in_sum[y]
        for o in range(1, Y):
            sums = sums + in_y[o - 1]
        rin[x, pl.ds(pl.multiple_of(y * TCH, 16), TCH)] = sums[0:TCH].astype(BF16)
        span = pl.ds(pl.multiple_of(y * TCH, 16), TCH)
        rin_query[x] = sums[TCH:CH].astype(BF16).astype(F32)
        return (
            [remote(rin.at[x, span], rin.at[x, span], dev(oy=o)) for o in range(1, Y)],
            [remote(rin_query.at[x], rin_query.at[x], dev(ox=o)) for o in range(1, X)],
        )

    in_copies, in_queries = in_middle()
    meets = []
    for p, (first, size) in enumerate(PARTS):
        span = pl.ds(first, size)
        hops[3][p].wait_recv()
        rest = part[rows(z * CH + first, size)] + swap[0, span]
        own[span] = ringbuf[3, span] + jnp.where(k == 1, rest, 0.0)
        meets.append(remote(own.at[span], own_other.at[span], sibling))

    def chunk_rows(o, first=0, size=TCH):
        return pl.ds(pl.multiple_of(((z - turn * o + 2 * Z) % Z) * TCH + first, 16), size)

    spread = {}
    for p, (first, size) in enumerate(PARTS):
        span = pl.ds(first, size)
        meets[p].wait_recv()
        full = own[span] + own_other[span]
        if size > 16:
            rquery[...] = full[16:24].astype(BF16).astype(F32)
        where = chunk_rows(0, first, 16)
        rout[where] = full[0:16].astype(BF16)
        for o in (3, 2, 1):
            spread[o, p] = remote(rout.at[where], rout.at[where], dev(oz=turn * o))

    for copy in in_queries:
        copy.wait_recv()
    query_columns = jnp.transpose(rquery[...])
    for q in range(QUERIES):
        column = query_columns[:, q:q + 1]
        for t in range(X):
            cols = slice(t * 128, t * 128 + 128)
            precond[q, :, cols] = (column * rin_query[t, q:q + 1] * inverse[:, cols]).astype(BF16)

    for copy in in_copies:
        copy.wait_recv()
    in_right = remote(rin.at[x], rin.at[x], dev(ox=1))
    in_left = remote(rin.at[x], rin.at[x], dev(ox=-1))

    far = []
    for p, (first, _) in enumerate(PARTS):
        core = 0 if p < 2 else 1
        spread[3, p].wait_recv()
        where = chunk_rows(3, first, 16)
        copy = remote(rout.at[where], rout.at[where], dev(oz=turn), start=False)
        far.append((core, first, 16, copy))

        @pl.when(k == core)
        def _():
            copy.start()
        spread[2, p].wait_recv()
        spread[1, p].wait_recv()
        if p == 1:
            in_right.wait_recv()
            in_cross = [
                remote(rin.at[left, pl.ds(0, 192)], rin.at[left, pl.ds(0, 192)], dev(ox=1)),
            ]
            in_left.wait_recv()
            in_cross += [
                remote(rin.at[right, pl.ds(192, 192)], rin.at[right, pl.ds(192, 192)], dev(ox=-1)),
            ]
    relayed = [remote(rout.at[chunk_rows(o)], rout.at[chunk_rows(o)], sibling) for o in (1, 2, 3)]
    late = []
    for core, first, size, copy in far:
        relay = remote(
            rout.at[chunk_rows(4, first, size)], rout.at[chunk_rows(4, first, size)], sibling, start=False
        )
        late.append((core, copy, relay))

        @pl.when(k == core)
        def _():
            copy.wait_recv()
            relay.start()
    for copy in in_cross + relayed:
        copy.wait_recv()
    for core, copy, relay in late:
        @pl.when(k != core)
        def _():
            relay.wait_recv()

    lanes = lax.broadcasted_iota(jnp.int32, (TRAIN, 128), 1)
    collected = jnp.zeros((TRAIN, 128), F32)
    for q in range(QUERIES):
        total = jnp.zeros((TRAIN, 128), F32)
        for at in range(0, X, 2):
            mixed = jnp.dot(
                rout[...], precond[q, :, at * 128:at * 128 + 256], preferred_element_type=F32
            )
            for n, t in enumerate((at, at + 1)):
                total = total + mixed[:, n * 128:n * 128 + 128] * rin[t].astype(F32)
        collected = jnp.where(lanes == q, jnp.sum(total, axis=1, keepdims=True), collected)
    scores = jnp.transpose(collected)[0:QUERIES]

    assert used[0] + 25 <= N_SEM
    fin = sum_start(fin_s, k, scores, [sibling])
    fin = sum_start(fin_z, z, sum_end(fin_s, fin), to_z)
    fin = sum_start(fin_y, y, sum_end(fin_z, fin), to_y)
    fin = sum_start(fin_x, x, sum_end(fin_y, fin), to_x)
    out[...] = sum_end(fin_x, fin)

    for copy in pending:
        copy.wait_send()

    @pl.when(k == 0)
    def _():
        for copy in hops[0]:
            copy.wait_send()
    for core, copy, relay in late:
        @pl.when(k == core)
        def _():
            copy.wait_send()
            relay.wait_send()


def per_device(grads_out, acts, query_index, train_index, out_basis, in_basis, eig_products):
    vmem = pl.BlockSpec(memory_space=pltpu.VMEM)
    hbm = pl.BlockSpec(memory_space=pl.ANY)
    scores = pl.pallas_call(
        kernel,
        out_shape=jax.ShapeDtypeStruct((QUERIES, TRAIN), F32),
        in_specs=[vmem, pl.BlockSpec(memory_space=pltpu.SMEM)] + [hbm] * 5,
        out_specs=vmem,
        scratch_shapes=[
            pltpu.VMEM((PICKS, 1), jnp.int32),
            pltpu.VMEM((POOL, CA), BF16),
            pltpu.VMEM((POOL, CB), BF16),
            pltpu.VMEM((POOL, 256), BF16),
            pltpu.VMEM((PICKS, CB), F32),
            pltpu.VMEM((PICKS, POOL), BF16),
            pltpu.VMEM((PICKS, POOL), BF16),
            pltpu.VMEM((PICKS, POOL), BF16),
            pltpu.VMEM((CA + CB, IB), BF16),
            pltpu.VMEM((256, JB), BF16),
            pltpu.VMEM((IB, JB), BF16),
            pltpu.VMEM((IB, JB), F32),
            pltpu.VMEM((PICKS, CA + CB), BF16),
            pltpu.VMEM((Z * CH, IB), F32),
            pltpu.VMEM((4, CH, IB), F32),
            pltpu.VMEM((4, CH, IB), F32),
            pltpu.VMEM((4, CH, IB), F32),
            pltpu.VMEM((CH, IB), F32),
            pltpu.VMEM((CH, IB), F32),
            pltpu.VMEM((TRAIN, IB), BF16),
            pltpu.VMEM((QUERIES, IB), F32),
            pltpu.VMEM((X, PICKS, 128), F32),
            pltpu.VMEM((2, PICKS // 2, 128), F32),
            pltpu.VMEM((2, PICKS // 2, 128), F32),
            pltpu.VMEM((2, PICKS, 128), F32),
            pltpu.VMEM((Y, CH, 128), F32),
            pltpu.VMEM((Y - 1, CH, 128), F32),
            pltpu.VMEM((X, TRAIN, 128), BF16),
            pltpu.VMEM((X, QUERIES, 128), F32),
            pltpu.VMEM((QUERIES, IB, JB), BF16),
            pltpu.VMEM((2, 8, 128), F32),
            pltpu.VMEM((Z, 8, 128), F32),
            pltpu.VMEM((Y, 8, 128), F32),
            pltpu.VMEM((X, 8, 128), F32),
            pltpu.VMEM((2, QUERIES, TRAIN), F32),
            pltpu.VMEM((Z, QUERIES, TRAIN), F32),
            pltpu.VMEM((Y, QUERIES, TRAIN), F32),
            pltpu.VMEM((X, QUERIES, TRAIN), F32),
            pltpu.SemaphoreType.DMA((N_SEM,)),
            pltpu.SemaphoreType.DMA((N_SEM,)),
            pltpu.SemaphoreType.DMA((6,)),
        ],
        compiler_params=pltpu.CompilerParams(
            collective_id=0, has_side_effects=True, vmem_limit_bytes=56 * 2**20
        ),
    )(train_index, query_index, grads_out, acts, out_basis, in_basis, eig_products)
    return scores * (1.0 / math.sqrt(DOUT * DIN))


def solution(mesh):
    in_specs = (
        P("row", "col"),
        P("col", "row"),
        P(),
        P(),
        P("col", "row"),
        P("row", "col"),
        P("row", "col"),
    )
    return jax.shard_map(
        per_device, mesh=mesh, in_specs=in_specs, out_specs=P(), check_vma=False
    )
```

```python
import math

import jax
import jax.numpy as jnp
from jax import lax
from jax.experimental import pallas as pl
from jax.experimental.pallas import tpu as pltpu
from jax.sharding import PartitionSpec as P

DOUT = 28672
DIN = 8192
QUERIES = 8
TRAIN = 384
POOL = 1024
X, Y, Z = 4, 8, 8
PICKS = 400
CA = 768
CB = 1024
IB = 896
JB = 512
TCH = 48
CH = 56
MESH = pl.DeviceIdType.MESH
F32 = jnp.float32
BF16 = jnp.bfloat16
FAR8 = (4, 3, 5, 2, 6, 1, 7)
FAR4 = (2, 1, 3)
PARTS = ((0, 16), (16, 16), (32, 24))
N_SEM = 208
ORDER = (
    ('A', 0, 1), ('A', 0, 3), ('B', 1), ('B', -1), ('Bx', 0, -1), ('eig',), ('A', 0, 2), ('Bx', 0, 1),
    ('B', 2), ('B', -2), ('A', 1, 0), ('A', -1, 0), ('damp_z',), ('A', 1, 1), ('A', -1, 1), ('Bx', 1, 1),
    ('Bx', 1, -1), ('A', 1, 3), ('A', -1, 3), ('hot_c',), ('Bx', -1, 1), ('Bx', -1, -1), ('hot_b',),
    ('A', 1, 2), ('A', -1, 2), ('Bxx', 0), ('acts',), ('Bx', 2, -1), ('B', 3), ('B', -3), ('Bx', 2, 1),
    ('Bx', -2, -1), ('damp_y',), ('B', 4), ('B', -4), ('Bx', -2, 1), ('A', 2, 0), ('A', -2, 0), ('A', 2, 1),
    ('A', -2, 1), ('Bxx', 1), ('in_rot',), ('Bxx', -1), ('A', 2, 3), ('A', -2, 3), ('A', 2, 2), ('A', -2, 2),
    ('hot_a',), ('Bx', 3, 1), ('pick_b', 0), ('Bx', 3, -1), ('Bx', -3, 1), ('Bx', -3, -1), ('A', 3, 0),
    ('A', -3, 0), ('Bxx', 2), ('Bxx', -2), ('A', 3, 1), ('A', -3, 1), ('Bx', 4, 1), ('Bx', 4, -1),
    ('damp_x',), ('A', 3, 3), ('Bx', -4, 1), ('Bx', -4, -1), ('pick_b', 1), ('pick_b', 3), ('A', -3, 3),
    ('A', 3, 2), ('A', -3, 2), ('Bxx', 3), ('in_x',), ('A', 4, 0), ('A', -4, 0), ('Bxx', -3), ('A', 4, 1),
    ('A', -4, 1), ('Bxx', 4), ('A', 4, 3), ('A', -4, 3), ('Bxx', -4), ('A', 4, 2), ('A', -4, 2),
)


def kernel(
    train_index, query_index, grads, acts, out_basis, in_basis, eig, out,
    want_rows, pool_a, pool_b, pool_c, sum_b, hot_a, hot_b, hot_c, obv, ibv, eigv, inverse, picked,
    part, swap, ringbuf, sendbuf, own, own_other, rout, rquery,
    in_part, in_relay, in_send, in_x, in_sum, in_y, rin, rin_query, precond, mixed, damp_s, damp_z, damp_y, damp_x,
    fin_s, fin_z, fin_y, fin_x, send_sems, recv_sems, load_sems,
):
    row = lax.axis_index("row")
    col = lax.axis_index("col")
    x, y = row // Y, row % Y
    z, k = col // 2, col % 2
    other = 1 - k
    turn = 1 - 2 * k

    def dev(ox=0, oy=0, oz=0):
        return (((x + ox + X) % X) * Y + (y + oy + Y) % Y, ((z + oz + Z) % Z) * 2 + k)

    sibling = (row, z * 2 + other)
    used = [0]
    pending = []

    def remote(src, dst, target, start=True):
        at = used[0]
        used[0] += 1
        copy = pltpu.make_async_remote_copy(
            src_ref=src, dst_ref=dst, send_sem=send_sems.at[at], recv_sem=recv_sems.at[at],
            device_id=target, device_id_type=MESH,
        )
        if start:
            copy.start()
            pending.append(copy)
        return copy

    def rows(start, size):
        return pl.ds(pl.multiple_of(start, 8), size)

    barrier = pltpu.get_barrier_semaphore()
    partners = [dev(oz=o) for o in FAR8] + [dev(oy=o) for o in FAR8] + [dev(ox=o) for o in FAR4]
    partners += [sibling]
    for partner in partners:
        pl.semaphore_signal(barrier, inc=1, device_id=partner, device_id_type=MESH)

    def at_a(px, py):
        return pl.ds(pl.multiple_of(((py + Y) % Y) * 128 + ((px + X) % X) * 32, 32), 32)

    def at_b(px, py, size=32, skip=0):
        return pl.ds(pl.multiple_of(((px + X) % X) * 256 + ((py + Y) % Y) * 32 + skip, 16), size)

    own_c = pl.ds(pl.multiple_of(k * 512 + z * 64, 64), 64)
    loads = [
        pltpu.make_async_copy(grads.at[:, pl.ds(CA, CB)], pool_b.at[at_b(x, y)], load_sems.at[0]),
        pltpu.make_async_copy(grads.at[:, pl.ds(0, CA)], pool_a.at[at_a(x, y)], load_sems.at[1]),
        pltpu.make_async_copy(acts, pool_c.at[own_c], load_sems.at[2]),
        pltpu.make_async_copy(eig, eigv, load_sems.at[3]),
        pltpu.make_async_copy(in_basis, ibv, load_sems.at[4]),
        pltpu.make_async_copy(out_basis, obv, load_sems.at[5]),
    ]
    for load in loads[:4]:
        load.start()

    @pl.when(k == 1)
    def _():
        ringbuf[0] = jnp.zeros((CH, IB), F32)

    for load in loads[:3]:
        load.wait()
    pl.semaphore_wait(barrier, len(partners))

    coming = {}

    def go(event, buf, where, **to):
        coming[event] = remote(buf.at[where], buf.at[where], dev(**to))

    def block_b(px, d):
        if abs(d) == 4:
            return at_b(px, y - 4, 16, 0 if d > 0 else 16)
        return at_b(px, y - d)

    def on_b(d):
        if abs(d) == 2:
            s = d // 2
            go(("B", 3 * s), pool_b, at_b(x, y - d), oy=s)
            go(("B", 4 * s), pool_b, at_b(x, y - d, 16, 0 if s > 0 else 16), oy=2 * s)
        go(("Bx", d, 1), pool_b, block_b(x, d), ox=1)
        go(("Bx", d, -1), pool_b, block_b(x, d), ox=-1)

    def on_bx(d, s):
        if (s > 0) == (d in (0, 1, 2, 3)):
            go(("Bxx", d), pool_b, block_b(x - s, d), ox=s)

    def on_a(d, o):
        where = at_a(x - o, y - d)
        if d == 0:
            go(("A", 1, o), pool_a, where, oy=1)
            go(("A", -1, o), pool_a, where, oy=-1)
        elif abs(d) < 3:
            s = 1 if d > 0 else -1
            go(("A", d + s, o), pool_a, where, oy=s)
        elif abs(d) == 3 and (d > 0) == (o < 2):
            s = d // 3
            go(("A", 4 * s, o), pool_a, where, oy=s)

    go(("B", 1), pool_b, at_b(x, y), oy=1)
    go(("B", -1), pool_b, at_b(x, y), oy=-1)
    for o in (1, 3, 2):
        go(("A", 0, o), pool_a, at_a(x, y), ox=o)
    go(("B", 2), pool_b, at_b(x, y), oy=2)
    go(("B", -2), pool_b, at_b(x, y), oy=-2)
    on_a(0, 0)
    go(("Bx", 0, 1), pool_b, at_b(x, y), ox=1)
    go(("Bx", 0, -1), pool_b, at_b(x, y), ox=-1)
    c_z = [remote(pool_c.at[own_c], pool_c.at[own_c], dev(oz=o)) for o in (1, 7, 2, 6, 3, 5, 4)]
    for load in loads[4:]:
        load.start()

    def sum_start(buf, me, value, targets):
        buf[me] = value
        return [remote(buf.at[me], buf.at[me], target) for target in targets]

    def sum_end(buf, copies):
        for copy in copies:
            copy.wait_recv()
        result = buf[0]
        for at in range(1, buf.shape[0]):
            result = result + buf[at]
        return result

    to_z = [dev(oz=o) for o in FAR8]
    to_y = [dev(oy=o) for o in FAR8]
    to_x = [dev(ox=o) for o in FAR4]

    train_line = jnp.broadcast_to(train_index[...].reshape(1, TRAIN).astype(F32), (8, TRAIN))
    want_rows[0:TRAIN] = jnp.transpose(train_line)[:, 0:1].astype(jnp.int32)
    lines = lax.broadcasted_iota(jnp.int32, (PICKS - TRAIN, 1), 0)
    query_rows = jnp.full((PICKS - TRAIN, 1), -1, jnp.int32)
    for q in range(QUERIES):
        query_rows = jnp.where(lines == q, query_index[q], query_rows)
    want_rows[TRAIN:PICKS] = query_rows

    def mark(hot, order):
        place = lax.broadcasted_iota(jnp.int32, (PICKS, POOL), 1)
        hot[...] = (order(place) == want_rows[...]).astype(F32).astype(BF16)

    def pick_b(o, last=False):
        group = pl.ds(pl.multiple_of(((x + X - o) % X) * 256, 256), 256)
        for at in range(0, CB, 256):
            some = jnp.dot(hot_b[:, group], pool_b[group, at:at + 256], preferred_element_type=F32)
            if o > 0:
                some = some + sum_b[:, at:at + 256]
            if last:
                picked[:, CA + at:CA + at + 256] = some.astype(BF16)
            else:
                sum_b[:, at:at + 256] = some

    half = PICKS // 2
    low, high = pl.ds(0, half), pl.ds(half, half)
    right, left, across = (x + 1) % X, (x + 3) % X, (x + 2) % X
    for event in ORDER:
        if event in coming:
            coming[event].wait_recv()
        kind = event[0]
        if kind == "A":
            on_a(*event[1:])
        elif kind == "B":
            on_b(*event[1:])
        elif kind == "Bx":
            on_bx(*event[1:])
        elif kind == "eig":
            loads[3].wait()
            total = jnp.zeros((8, 128), F32)
            for at in range(0, IB, 128):
                block = eigv[at:at + 128, :].astype(F32)
                for at_lane in range(0, JB, 128):
                    total = total + jnp.sum(block[:, at_lane:at_lane + 128].reshape(16, 8, 128), axis=0)
            damp = sum_start(damp_s, k, total, [sibling])
        elif kind == "hot_a":
            mark(hot_a, lambda at: ((at // 32) % 4) * 256 + (at // 128) * 32 + at % 32)
        elif kind == "hot_b":
            mark(hot_b, lambda at: at)
        elif kind == "hot_c":
            mark(hot_c, lambda at: ((at // 64) % 8) * 128 + (at // 512) * 64 + at % 64)
        elif kind == "pick_b":
            pick_b(event[1])
        elif kind == "damp_z":
            damp = sum_start(damp_z, z, sum_end(damp_s, damp), to_z)
        elif kind == "damp_y":
            damp = sum_start(damp_y, y, sum_end(damp_z, damp), to_y)
        elif kind == "damp_x":
            damp = sum_start(damp_x, x, sum_end(damp_y, damp), to_x)
        elif kind == "acts":
            for copy in c_z:
                copy.wait_recv()
            half_c = pl.ds(pl.multiple_of(k * 512, 512), 512)
            c_s = remote(pool_c.at[half_c], pool_c.at[half_c], sibling)
        elif kind == "in_rot":
            c_s.wait_recv()
            loads[4].wait()
            act_rows = jnp.dot(hot_c[...], pool_c[...], preferred_element_type=F32).astype(BF16)
            for at in range(X):
                in_part[at] = jnp.dot(
                    act_rows, ibv[:, at * 128:at * 128 + 128], preferred_element_type=F32
                )
        elif kind == "in_x":
            relays = [
                remote(in_part.at[across, low], in_relay.at[0], dev(ox=1)),
                remote(in_part.at[across, high], in_relay.at[1], dev(ox=-1)),
            ]
            in_copies = [
                remote(in_part.at[right, high], in_x.at[0, high], dev(ox=1)),
                remote(in_part.at[left, low], in_x.at[1, low], dev(ox=-1)),
            ]

    for at in range(0, CA, 256):
        picked[:, at:at + 256] = jnp.dot(
            hot_a[...], pool_a[:, at:at + 256], preferred_element_type=F32
        ).astype(BF16)
    pick_b(2, last=True)
    for copy in relays:
        copy.wait_recv()
    in_send[0] = in_relay[0] + in_part[right, low]
    in_send[1] = in_relay[1] + in_part[left, high]
    in_copies += [
        remote(in_send.at[0], in_x.at[0, low], dev(ox=1)),
        remote(in_send.at[1], in_x.at[1, high], dev(ox=-1)),
    ]

    def chunk(d):
        return rows(((d + 2 * Z) % Z) * CH, CH)

    loads[5].wait()
    swaps = [[] for _ in range(4)]
    for start, end in ((0, 512), (512, IB)):
        for at in range(start, end, 256):
            width = min(256, IB - at)
            rotated = jnp.dot(picked[...], obv[:, at:at + width], preferred_element_type=F32)
            for d in range(Z):
                part[d * CH:d * CH + TCH, at:at + width] = rotated[d * TCH:d * TCH + TCH]
                part[d * CH + TCH:d * CH + CH, at:at + width] = rotated[TRAIN:TRAIN + QUERIES]
        span = pl.ds(start, end - start)
        for j in range(4):
            need = jnp.where(k == 1, z + 4 - j, z if j == 0 else z - 4 + j)
            swaps[j].append(remote(part.at[chunk(need), span], swap.at[j, :, span], sibling))

    hops = []
    for s in range(4):
        for copy in swaps[s]:
            copy.wait_recv()
        mine = part.at[chunk(z + turn * (4 - s))]
        hop = []
        for p, (first, size) in enumerate(PARTS):
            span = pl.ds(first, size)
            if s > 0:
                if s == 1:
                    @pl.when(k == 0)
                    def _():
                        hops[0][p].wait_recv()
                else:
                    hops[s - 1][p].wait_recv()
                sendbuf[s, span] = mine[span] + swap[s, span] + ringbuf[s - 1, span]
            else:
                sendbuf[s, span] = mine[span] + swap[s, span]
            copy = remote(
                sendbuf.at[s, span], ringbuf.at[s, span], dev(oz=turn), start=s > 0
            )
            if s == 0:
                @pl.when(k == 0)
                def _():
                    copy.start()
            hop.append(copy)
        hops.append(hop)
        if s == 0:
            for copy in in_copies:
                copy.wait_recv()
            sums = in_part[x] + in_x[0] + in_x[1]
            for d in range(Y):
                in_sum[d, 0:TCH] = sums[d * TCH:d * TCH + TCH]
                in_sum[d, TCH:CH] = sums[TRAIN:TRAIN + QUERIES]
            in_copies = [
                remote(in_sum.at[(y + o) % Y], in_y.at[o - 1], dev(oy=o)) for o in FAR8
            ]
        if s == 2:
            damping = 0.1 * jnp.sum(sum_end(damp_x, damp)) / (DOUT * DIN)
            inverse[...] = 1.0 / (eigv[...].astype(F32) + damping)

    def in_middle():
        for copy in in_copies:
            copy.wait_recv()
        sums = in_sum[y]
        for o in range(1, Y):
            sums = sums + in_y[o - 1]
        rin[x, pl.ds(pl.multiple_of(y * TCH, 16), TCH)] = sums[0:TCH].astype(BF16)
        span = pl.ds(pl.multiple_of(y * TCH, 16), TCH)
        rin_query[x] = sums[TCH:CH].astype(BF16).astype(F32)
        return (
            [remote(rin.at[x, span], rin.at[x, span], dev(oy=o)) for o in FAR8],
            [remote(rin_query.at[x], rin_query.at[x], dev(ox=o)) for o in FAR4],
        )

    in_copies, in_queries = in_middle()
    meets = []
    for p, (first, size) in enumerate(PARTS):
        span = pl.ds(first, size)
        hops[3][p].wait_recv()
        rest = part[rows(z * CH + first, size)] + swap[0, span]
        own[span] = ringbuf[3, span] + jnp.where(k == 1, rest, 0.0)
        meets.append(remote(own.at[span], own_other.at[span], sibling))

    def chunk_rows(o, first=0, size=TCH):
        return pl.ds(pl.multiple_of(((z - turn * o + 2 * Z) % Z) * TCH + first, 16), size)

    spread = {}
    for p, (first, size) in enumerate(PARTS):
        span = pl.ds(first, size)
        meets[p].wait_recv()
        full = own[span] + own_other[span]
        if size > 16:
            rquery[...] = full[16:24].astype(BF16).astype(F32)
        where = chunk_rows(0, first, 16)
        rout[where] = full[0:16].astype(BF16)
        for o in (3, 2, 1):
            spread[o, p] = remote(rout.at[where], rout.at[where], dev(oz=turn * o))

    for copy in in_queries:
        copy.wait_recv()
    query_columns = jnp.transpose(rquery[...])
    for q in range(QUERIES):
        column = query_columns[:, q:q + 1]
        for t in range(X):
            cols = slice(t * 128, t * 128 + 128)
            precond[q, :, cols] = (column * rin_query[t, q:q + 1] * inverse[:, cols]).astype(BF16)

    for copy in in_copies:
        copy.wait_recv()
    in_right = remote(rin.at[x], rin.at[x], dev(ox=1))
    in_left = remote(rin.at[x], rin.at[x], dev(ox=-1))

    far = []
    for p, (first, _) in enumerate(PARTS):
        core = 0 if p < 2 else 1
        spread[3, p].wait_recv()
        where = chunk_rows(3, first, 16)
        copy = remote(rout.at[where], rout.at[where], dev(oz=turn), start=False)
        far.append((core, first, 16, copy))

        @pl.when(k == core)
        def _():
            copy.start()
        spread[2, p].wait_recv()
        spread[1, p].wait_recv()
    relayed = [remote(rout.at[chunk_rows(o)], rout.at[chunk_rows(o)], sibling) for o in (1, 2, 3)]
    in_right.wait_recv()
    in_cross = [
        remote(rin.at[left, pl.ds(0, 192)], rin.at[left, pl.ds(0, 192)], dev(ox=1)),
    ]
    in_left.wait_recv()
    in_cross += [
        remote(rin.at[right, pl.ds(192, 192)], rin.at[right, pl.ds(192, 192)], dev(ox=-1)),
    ]
    late = []
    for core, first, size, copy in far:
        relay = remote(
            rout.at[chunk_rows(4, first, size)], rout.at[chunk_rows(4, first, size)], sibling, start=False
        )
        late.append((core, copy, relay))

        @pl.when(k == core)
        def _():
            copy.wait_recv()
            relay.start()
    for copy in relayed:
        copy.wait_recv()
    for core, copy, relay in late:
        @pl.when(k != core)
        def _():
            relay.wait_recv()

    for q in range(QUERIES):
        for at in range(0, JB, 256):
            mixed[q, :, at:at + 256] = jnp.dot(
                rout[...], precond[q, :, at:at + 256], preferred_element_type=F32
            )
    for copy in in_cross:
        copy.wait_recv()
    lanes = lax.broadcasted_iota(jnp.int32, (TRAIN, 128), 1)
    collected = jnp.zeros((TRAIN, 128), F32)
    for q in range(QUERIES):
        total = jnp.zeros((TRAIN, 128), F32)
        for t in range(X):
            total = total + mixed[q, :, t * 128:t * 128 + 128] * rin[t].astype(F32)
        collected = jnp.where(lanes == q, jnp.sum(total, axis=1, keepdims=True), collected)
    scores = jnp.transpose(collected)[0:QUERIES]

    assert used[0] + 25 <= N_SEM
    fin = sum_start(fin_s, k, scores, [sibling])
    fin = sum_start(fin_z, z, sum_end(fin_s, fin), to_z)
    fin = sum_start(fin_y, y, sum_end(fin_z, fin), to_y)
    fin = sum_start(fin_x, x, sum_end(fin_y, fin), to_x)
    out[...] = sum_end(fin_x, fin)

    for copy in pending:
        copy.wait_send()

    @pl.when(k == 0)
    def _():
        for copy in hops[0]:
            copy.wait_send()
    for core, copy, relay in late:
        @pl.when(k == core)
        def _():
            copy.wait_send()
            relay.wait_send()


def per_device(grads_out, acts, query_index, train_index, out_basis, in_basis, eig_products):
    vmem = pl.BlockSpec(memory_space=pltpu.VMEM)
    hbm = pl.BlockSpec(memory_space=pl.ANY)
    scores = pl.pallas_call(
        kernel,
        out_shape=jax.ShapeDtypeStruct((QUERIES, TRAIN), F32),
        in_specs=[vmem, pl.BlockSpec(memory_space=pltpu.SMEM)] + [hbm] * 5,
        out_specs=vmem,
        scratch_shapes=[
            pltpu.VMEM((PICKS, 1), jnp.int32),
            pltpu.VMEM((POOL, CA), BF16),
            pltpu.VMEM((POOL, CB), BF16),
            pltpu.VMEM((POOL, 256), BF16),
            pltpu.VMEM((PICKS, CB), F32),
            pltpu.VMEM((PICKS, POOL), BF16),
            pltpu.VMEM((PICKS, POOL), BF16),
            pltpu.VMEM((PICKS, POOL), BF16),
            pltpu.VMEM((CA + CB, IB), BF16),
            pltpu.VMEM((256, JB), BF16),
            pltpu.VMEM((IB, JB), BF16),
            pltpu.VMEM((IB, JB), F32),
            pltpu.VMEM((PICKS, CA + CB), BF16),
            pltpu.VMEM((Z * CH, IB), F32),
            pltpu.VMEM((4, CH, IB), F32),
            pltpu.VMEM((4, CH, IB), F32),
            pltpu.VMEM((4, CH, IB), F32),
            pltpu.VMEM((CH, IB), F32),
            pltpu.VMEM((CH, IB), F32),
            pltpu.VMEM((TRAIN, IB), BF16),
            pltpu.VMEM((QUERIES, IB), F32),
            pltpu.VMEM((X, PICKS, 128), F32),
            pltpu.VMEM((2, PICKS // 2, 128), F32),
            pltpu.VMEM((2, PICKS // 2, 128), F32),
            pltpu.VMEM((2, PICKS, 128), F32),
            pltpu.VMEM((Y, CH, 128), F32),
            pltpu.VMEM((Y - 1, CH, 128), F32),
            pltpu.VMEM((X, TRAIN, 128), BF16),
            pltpu.VMEM((X, QUERIES, 128), F32),
            pltpu.VMEM((QUERIES, IB, JB), BF16),
            pltpu.VMEM((QUERIES, TRAIN, JB), F32),
            pltpu.VMEM((2, 8, 128), F32),
            pltpu.VMEM((Z, 8, 128), F32),
            pltpu.VMEM((Y, 8, 128), F32),
            pltpu.VMEM((X, 8, 128), F32),
            pltpu.VMEM((2, QUERIES, TRAIN), F32),
            pltpu.VMEM((Z, QUERIES, TRAIN), F32),
            pltpu.VMEM((Y, QUERIES, TRAIN), F32),
            pltpu.VMEM((X, QUERIES, TRAIN), F32),
            pltpu.SemaphoreType.DMA((N_SEM,)),
            pltpu.SemaphoreType.DMA((N_SEM,)),
            pltpu.SemaphoreType.DMA((6,)),
        ],
        compiler_params=pltpu.CompilerParams(
            collective_id=0, has_side_effects=True, vmem_limit_bytes=56 * 2**20
        ),
    )(train_index, query_index, grads_out, acts, out_basis, in_basis, eig_products)
    return scores * (1.0 / math.sqrt(DOUT * DIN))


def solution(mesh):
    in_specs = (
        P("row", "col"),
        P("col", "row"),
        P(),
        P(),
        P("col", "row"),
        P("row", "col"),
        P("row", "col"),
    )
    return jax.shard_map(
        per_device, mesh=mesh, in_specs=in_specs, out_specs=P(), check_vma=False
    )
```
